512 devices in a mesh: mp: 8 (over z_hi, core), feat: 64 (over z_lo, x, y).
Axes of the slice: x: 4, y: 8, z: 8 (z_hi: 4, z_lo: 2; z = z_hi * 2 + z_lo), core: 2. Of those that a mesh axis runs over, the one named last changes fastest.
Arguments:
- residual: bfloat16 [2, 384, 2304], P(None, 'feat', 'mp'), may hold values from -6 to 6
- norm_gain: float32 [2, 2304], P(None, 'mp'), may hold values from 0.1 to 1.9
- gate_weight: bfloat16 [2, 2304, 9216], P(None, 'mp', 'feat'), may hold values from -0.125 to 0.125
- up_weight: bfloat16 [2, 2304, 9216], P(None, 'mp', 'feat'), may hold values from -0.125 to 0.125
- down_weight: bfloat16 [2, 9216, 2304], P(None, 'feat', 'mp'), may hold values from -0.0625 to 0.0625
- encoder: bfloat16 [2, 32768, 2304], P(None, 'feat', 'mp'), may hold values from -0.125 to 0.125
- encoder_bias: float32 [2, 32768], P(None, 'feat'), may hold values from -3 to 3
- decoder: bfloat16 [3, 32768, 2304], P(None, 'feat', 'mp'), may hold values from -0.03125 to 0.03125
Outputs:
- grad_encoder: bfloat16 [2, 32768, 2304], P(None, 'feat', 'mp')
- grad_bias: float32 [2, 32768], P(None, 'feat')
- grad_decoder: bfloat16 [3, 32768, 2304], P(None, 'feat', 'mp')
The draws below stay inside these ranges and needn't reach their ends.
All inputs are finite; a program needn't handle non-finite values.
Results may differ from the reference program's by a relative error of at most 0.02.
The reference program's roundings to bfloat16 on the way count: a program that leaves them out, or rounds other values in their place, can miss the bound.
Values may be sent and summed in bfloat16 or wider, within the bound.
A program may use at most 64 MiB of HBM per device.

```python
import math
import jax
import jax.numpy as jnp
from jax import lax

D = 2304
FF = 9216
F = 32768
TOKENS = 384


def steps_of(rng, dims, pieces, smallest, top_value):
    def one(axis_at, shards_of):
        draws = jax.random.uniform(jax.random.fold_in(jax.random.fold_in(rng, 6), axis_at), (shards_of,), jnp.float32, smallest / len(pieces), top_value / len(pieces))
        return jnp.repeat(jnp.exp(draws), dims[axis_at] // shards_of).reshape((-1,) + (1,) * (len(dims) - axis_at - 1))

    loudness = one(*pieces[0])
    for cut in pieces[1:]:
        loudness = loudness * one(*cut)
    return loudness


def gaussian(rng, shape, deviation, limit, pieces=(), held_as=jnp.bfloat16):
    drawn = deviation * jax.random.normal(rng, shape, jnp.float32)
    if pieces:
        drawn = drawn * steps_of(rng, shape, pieces, -0.22, 0.18)
    return jnp.clip(drawn, -limit, limit).astype(held_as)


def setup_inputs(seed: int = 0) -> dict:
    keys = jax.random.split(jax.random.key(seed), 9)
    residual = gaussian(keys[0], (2, TOKENS, D), 1.0, 6.0, ((1, 64), (2, 8)))
    norm_gain = jnp.clip(1.0 + 0.18 * jax.random.normal(keys[1], (2, D), jnp.float32), 0.1, 1.9)
    gate_weight = gaussian(keys[2], (2, D, FF), D ** -0.5, 0.125, ((1, 8), (2, 64)))
    up_weight = gaussian(keys[3], (2, D, FF), D ** -0.5, 0.125, ((1, 8), (2, 64)))
    down_weight = gaussian(keys[4], (2, FF, D), FF ** -0.5, 0.0625, ((1, 64), (2, 8)))
    encoder = gaussian(keys[5], (2, F, D), D ** -0.5, 0.125, ((1, 64), (2, 8)))
    encoder_bias = gaussian(keys[6], (2, F), 0.5, 3.0, ((1, 64),), jnp.float32)
    decoder = gaussian(keys[7], (3, F, D), F ** -0.5, 0.03125, ((1, 64), (2, 8)))
    return dict(residual=residual, norm_gain=norm_gain, gate_weight=gate_weight, up_weight=up_weight, down_weight=down_weight, encoder=encoder, encoder_bias=encoder_bias, decoder=decoder)


sparsity_weight = 0.1

def outer_product(weights_side, errors_side):
    return jnp.dot(weights_side.T, errors_side, preferred_element_type=jnp.float32)

def reference(residual, norm_gain, gate_weight, up_weight, down_weight, encoder, encoder_bias, decoder):
    values = residual.astype(jnp.float32)
    mean_square = lax.optimization_barrier(jnp.mean(values * values, axis=2, keepdims=True))
    normed = (values * jax.lax.rsqrt(mean_square + 1e-06) * norm_gain[:, None, :]).astype(jnp.bfloat16)
    targets = []
    actives = []
    for layer_index in range(2):
        gate_part = jnp.dot(normed[layer_index], gate_weight[layer_index], preferred_element_type=jnp.float32)
        up_part = jnp.dot(normed[layer_index], up_weight[layer_index], preferred_element_type=jnp.float32)
        hidden = (jax.nn.gelu(gate_part, approximate=True) * up_part).astype(jnp.bfloat16)
        targets.append(jnp.dot(hidden, down_weight[layer_index], preferred_element_type=jnp.float32))
        preact = jnp.dot(normed[layer_index], encoder[layer_index].T, preferred_element_type=jnp.float32) + encoder_bias[layer_index][None, :]
        actives.append(jnp.maximum(preact, 0.0).astype(jnp.bfloat16))
    rebuilt_first = jnp.dot(actives[0], decoder[0], preferred_element_type=jnp.float32)
    rebuilt_second = jnp.dot(actives[0], decoder[1], preferred_element_type=jnp.float32) + jnp.dot(actives[1], decoder[2], preferred_element_type=jnp.float32)
    error_first = (rebuilt_first - targets[0]).astype(jnp.bfloat16)
    error_second = (rebuilt_second - targets[1]).astype(jnp.bfloat16)
    loss_scale = 1.0 / math.sqrt(TOKENS)
    back_first = jnp.dot(error_first, decoder[0].T, preferred_element_type=jnp.float32) + jnp.dot(error_second, decoder[1].T, preferred_element_type=jnp.float32)
    back_second = jnp.dot(error_second, decoder[2].T, preferred_element_type=jnp.float32)
    grad_first = jnp.where(actives[0] > 0, loss_scale * (back_first + sparsity_weight), 0.0).astype(jnp.bfloat16)
    grad_second = jnp.where(actives[1] > 0, loss_scale * (back_second + sparsity_weight), 0.0).astype(jnp.bfloat16)
    grad_encoder = jnp.stack([outer_product(grad_first, normed[0]), outer_product(grad_second, normed[1])]).astype(jnp.bfloat16)
    grad_bias = jnp.stack([lax.optimization_barrier(jnp.sum(grad_first.astype(jnp.float32), axis=0)), lax.optimization_barrier(jnp.sum(grad_second.astype(jnp.float32), axis=0))])
    grad_decoder = (loss_scale * jnp.stack([outer_product(actives[0], error_first), outer_product(actives[0], error_second), outer_product(actives[1], error_second)])).astype(jnp.bfloat16)
    return (grad_encoder, grad_bias, grad_decoder)
```

```python
import functools
import math

import jax
import jax.numpy as jnp
from jax import lax
from jax.experimental import pallas as pl
from jax.experimental.pallas import tpu as pltpu
from jax.sharding import PartitionSpec as P

MESH = pl.DeviceIdType.MESH
F32 = jnp.float32
BF16 = jnp.bfloat16
sparsity_weight = 0.1

STAGE_TIMES = (0, 2, 8, 13, 15, 20, 25, 30, 32, 37, 42, 44)
CHUNK_STEP = 9.0


def nt(a, b):
    return lax.dot_general(a, b, (((1,), (1,)), ((), ())), preferred_element_type=F32)


def tn(a, b):
    return lax.dot_general(a, b, (((0,), (0,)), ((), ())), preferred_element_type=F32)


def kernel(
    width, residual, gain, gate_w, up_w, down_w, encoder, bias, decoder,
    grad_encoder, grad_bias, grad_decoder,
    squares, padded, xl_block, own_block, normed, w_dec, w_enc, w_gate,
    pre_mine, pre_core, pre_z, pre_recv, gu_mine, gu_core, gu_z, gu_recv,
    act, err_part, err_recv, err_xl, errors, mask,
    back_mine, back_core, back_z, back_recv, grads, enc_sum,
    sems,
):
    layers, local, cols = residual.shape
    feats = encoder.shape[1]
    hid = gate_w.shape[2]
    chunks, slots, rows, _ = normed.shape
    chunk_tokens = slots * rows
    both = layers * feats
    tokens = chunks * chunk_tokens
    scale = 1.0 / math.sqrt(tokens)

    mp = lax.axis_index("mp")
    ft = lax.axis_index("feat")
    zh, core = mp // 2, mp % 2
    xl, yy = ft // 8, ft % 8
    mine = core * 4 + zh

    core_dev = (zh * 2 + 1 - core, ft)
    z_at = [(zh + d) % 4 for d in (1, 2, 3)]
    z_dev = [(z * 2 + core, ft) for z in z_at]
    far_dev = [(z * 2 + 1 - core, ft) for z in z_at]
    xl_at = [(xl + d) % 8 for d in range(1, 8)]
    xl_dev = [(mp, a * 8 + yy) for a in xl_at]
    y_at = [(yy + d) % 8 for d in range(1, 8)]
    y_dev = [(mp, xl * 8 + a) for a in y_at]
    partners = [core_dev] + z_dev + far_dev + xl_dev + y_dev

    pending = []

    def send(i, src, dst, dev):
        pltpu.make_async_remote_copy(
            src_ref=src, dst_ref=dst, send_sem=sems.at[0, i], recv_sem=sems.at[1, i],
            device_id=dev, device_id_type=MESH,
        ).start()

    def wait(side, i, ref):
        pltpu.make_async_copy(ref, ref, sems.at[side, i]).wait()

    barrier = pltpu.get_barrier_semaphore()
    for dev in partners:
        pl.semaphore_signal(barrier, inc=1, device_id=dev, device_id_type=MESH)

    values = [residual[l].astype(F32) for l in range(layers)]
    for l in range(layers):
        total = jnp.sum(values[l] * values[l], axis=1, keepdims=True)
        squares[mp, l] = jnp.zeros((8, 128), F32)
        squares[mp, l, 0:local, :] = jnp.broadcast_to(total, (local, 128))
    padded[...] = jnp.zeros_like(padded)

    pl.semaphore_wait(barrier, len(partners))

    for dev in z_dev + far_dev + [core_dev]:
        send(0, squares.at[mp], squares.at[mp], dev)
    pending.append((0, squares.at[0:7]))

    w_dec[...] = jnp.zeros_like(w_dec)
    w_dec[0:feats, 0:cols] = decoder[0]
    w_dec[0:feats, cols : 2 * cols] = decoder[1]
    w_dec[feats:both, cols : 2 * cols] = decoder[2]
    w_dec[both : both + hid, 0:cols] = down_w[0]
    w_dec[both + hid : both + 2 * hid, cols : 2 * cols] = down_w[1]
    w_enc[...] = jnp.zeros_like(w_enc)
    w_enc[0:feats, 0:cols] = encoder[0]
    w_enc[feats:both, cols : 2 * cols] = encoder[1]
    up_at = gu_mine.shape[3] - 2 * hid
    w_gate[...] = jnp.zeros_like(w_gate)
    for l in range(layers):
        w_gate[l * cols : (l + 1) * cols, l * hid : (l + 1) * hid] = gate_w[l]
        w_gate[l * cols : (l + 1) * cols, up_at + l * hid : up_at + (l + 1) * hid] = up_w[l]

    wait(1, 0, squares.at[0:7])
    for l in range(layers):
        total = squares[0, l]
        for m in range(1, 8):
            total = total + squares[m, l]
        inverse = lax.rsqrt(total[0:local, 0:1] / width + 1e-06)
        padded[0:local, l * cols : (l + 1) * cols] = values[l] * inverse * gain[l : l + 1, :]
    xl_block[xl] = padded[...].astype(BF16)
    for dev in xl_dev:
        send(1, xl_block.at[xl], xl_block.at[xl], dev)
    pending.append((1, xl_block.at[0:7]))
    wait(1, 1, xl_block.at[0:7])
    for s in range(8):
        own_block[s * local : (s + 1) * local, :] = xl_block[s].astype(F32)[0:local, :]
    for k in range(chunks):
        normed[k, yy] = own_block[k * rows : (k + 1) * rows, :].astype(BF16)
        for dev in y_dev:
            send(2 + k, normed.at[k, yy], normed.at[k, yy], dev)
        pending.append((2 + k, normed.at[k, 0:7]))

    def slot(kind, k):
        return 2 + chunks * (1 + kind) + k

    def pre_matmul(k):
        wait(1, 2 + k, normed.at[k, 0:7])
        x = normed[k].reshape(chunk_tokens, 2 * cols)
        pre_mine[k] = nt(x, w_enc[...]).reshape(slots, rows, both)
        send(slot(0, k), pre_mine.at[k, pl.ds((1 - core) * 4, 4)], pre_core.at[k], core_dev)
        pending.append((slot(0, k), pre_core.at[k]))
        gu = jnp.dot(x, w_gate[...], preferred_element_type=F32)
        gu_mine[k] = gu.astype(BF16).reshape(slots, rows, -1)
        send(slot(1, k), gu_mine.at[k, pl.ds((1 - core) * 4, 4)], gu_core.at[k], core_dev)
        pending.append((slot(1, k), gu_core.at[k]))

    def pre_to_z(k):
        wait(1, slot(0, k), pre_core.at[k])
        for z, dev in zip(z_at, z_dev):
            pre_z[k, z] = pre_mine[k, core * 4 + z] + pre_core[k, z]
            send(slot(2, k), pre_z.at[k, z], pre_recv.at[k, zh], dev)
        pending.append((slot(2, k), pre_z.at[k, 0:3]))
        pre_recv[k, zh] = pre_mine[k, mine] + pre_core[k, zh]
        wait(1, slot(1, k), gu_core.at[k])
        for z, dev in zip(z_at, z_dev):
            gu_z[k, z] = (gu_mine[k, core * 4 + z].astype(F32) + gu_core[k, z].astype(F32)).astype(BF16)
            send(slot(3, k), gu_z.at[k, z], gu_recv.at[k, zh], dev)
        pending.append((slot(3, k), gu_z.at[k, 0:3]))
        gu_recv[k, zh] = (gu_mine[k, mine].astype(F32) + gu_core[k, zh].astype(F32)).astype(BF16)

    def activate(k):
        wait(1, slot(2, k), pre_recv.at[k, 0:3])
        total = pre_recv[k, 0] + pre_recv[k, 1] + pre_recv[k, 2] + pre_recv[k, 3]
        for l in range(layers):
            act[k, mine, :, l * feats : (l + 1) * feats] = jnp.maximum(
                total[:, l * feats : (l + 1) * feats] + bias[l : l + 1, :], 0.0
            ).astype(BF16)
        wait(1, slot(3, k), gu_recv.at[k, 0:3])
        gu = gu_recv[k, 0].astype(F32)
        for z in range(1, 4):
            gu = gu + gu_recv[k, z].astype(F32)
        hidden = jax.nn.gelu(gu[:, 0 : 2 * hid], approximate=True) * gu[:, up_at : up_at + 2 * hid]
        act[k, mine, :, both : both + 2 * hid] = -hidden.astype(BF16)
        for dev in z_dev:
            send(slot(4, k), act.at[k, mine], act.at[k, mine], dev)
        pending.append((slot(4, k), act.at[k, 0:3]))

    def act_to_core(k):
        wait(1, slot(4, k), act.at[k, 0:3])
        half = act.at[k, pl.ds(core * 4, 4)]
        send(slot(5, k), half, half, core_dev)
        pending.append((slot(5, k), act.at[k, 0:4]))

    def rebuild(k):
        wait(1, slot(5, k), act.at[k, 0:4])
        a = act[k].reshape(chunk_tokens, -1)
        err_part[k] = (
            jnp.dot(a, w_dec[...], preferred_element_type=F32).astype(BF16).reshape(slots, rows, -1)
        )
        for s, dev in zip(y_at, y_dev):
            send(slot(6, k), err_part.at[k, s], err_recv.at[k, yy], dev)
        pending.append((slot(6, k), err_part.at[k, 0:7]))
        err_recv[k, yy] = err_part[k, yy]
        start = pl.multiple_of(mine * 128, 128)
        own = act[k, :, :, pl.ds(start, 128)].reshape(chunk_tokens, 128)
        mask[k] = own.astype(F32).T

    def sum_y(k):
        wait(1, slot(6, k), err_recv.at[k, 0:7])
        total = err_recv[k, 0].astype(F32)
        for s in range(1, 8):
            total = total + err_recv[k, s].astype(F32)
        err_xl[k, xl] = total.astype(BF16)
        for dev in xl_dev:
            send(slot(7, k), err_xl.at[k, xl], err_xl.at[k, xl], dev)
        pending.append((slot(7, k), err_xl.at[k, 0:7]))

    def sum_xl(k):
        wait(1, slot(7, k), err_xl.at[k, 0:7])
        total = err_xl[k, 0].astype(F32)
        for s in range(1, 8):
            total = total + err_xl[k, s].astype(F32)
        errors[k, yy] = total.astype(BF16)
        for dev in y_dev:
            send(slot(8, k), errors.at[k, yy], errors.at[k, yy], dev)
        pending.append((slot(8, k), errors.at[k, 0:7]))

    def back_matmul(k):
        wait(1, slot(8, k), errors.at[k, 0:7])
        e = errors[k].reshape(chunk_tokens, 2 * cols)
        back = nt(w_dec[0:both, :], e)
        back_mine[k] = back.astype(BF16).reshape(slots, both // slots, chunk_tokens)
        send(slot(9, k), back_mine.at[k, pl.ds((1 - core) * 4, 4)], back_core.at[k], core_dev)
        pending.append((slot(9, k), back_core.at[k]))

    def back_to_z(k):
        wait(1, slot(9, k), back_core.at[k])
        for z, dev in zip(z_at, z_dev):
            back_z[k, z] = (
                back_mine[k, core * 4 + z].astype(F32) + back_core[k, z].astype(F32)
            ).astype(BF16)
            send(slot(10, k), back_z.at[k, z], back_recv.at[k, zh], dev)
        pending.append((slot(10, k), back_z.at[k, 0:3]))
        back_recv[k, zh] = (
            back_mine[k, mine].astype(F32) + back_core[k, zh].astype(F32)
        ).astype(BF16)

    def pre_grad(k):
        wait(1, slot(10, k), back_recv.at[k, 0:3])
        total = back_recv[k, 0].astype(F32)
        for z in range(1, 4):
            total = total + back_recv[k, z].astype(F32)
        grads[k, mine] = jnp.where(
            mask[k] > 0, scale * (total + sparsity_weight), 0.0
        ).astype(BF16)
        for dev in z_dev:
            send(slot(11, k), grads.at[k, mine], grads.at[k, mine], dev)
        pending.append((slot(11, k), grads.at[k, 0:3]))

    def grads_to_core(k):
        wait(1, slot(11, k), grads.at[k, 0:3])
        half = grads.at[k, pl.ds(core * 4, 4)]
        send(slot(12, k), half, half, core_dev)
        pending.append((slot(12, k), grads.at[k, 0:4]))

    def encoder_grads(k):
        wait(1, slot(12, k), grads.at[k, 0:4])
        g = grads[k].reshape(both, chunk_tokens)
        x = normed[k].reshape(chunk_tokens, 2 * cols)
        ones = jnp.ones((8, chunk_tokens), BF16)
        for l in range(layers):
            part = jnp.dot(g[l * feats : (l + 1) * feats], x, preferred_element_type=F32)[
                :, l * cols : (l + 1) * cols
            ]
            if k > 0:
                part = part + enc_sum[l]
            if k < chunks - 1:
                enc_sum[l] = part
            else:
                grad_encoder[l] = part.astype(BF16)
            column = nt(ones, g[l * feats : (l + 1) * feats])[0:1]
            if k > 0:
                column = column + grad_bias[l : l + 1, :]
            grad_bias[l : l + 1, :] = column

    def decoder_grads():
        a = act[...].reshape(tokens, -1)
        e = errors[...].reshape(tokens, 2 * cols)
        first = scale * tn(a[:, 0:feats], e)
        grad_decoder[0] = first[:, 0:cols].astype(BF16)
        grad_decoder[1] = first[:, cols : 2 * cols].astype(BF16)
        second = scale * tn(a[:, feats:both], e)
        grad_decoder[2] = second[:, cols : 2 * cols].astype(BF16)

    stages = (
        pre_matmul, pre_to_z, activate, act_to_core, rebuild, sum_y, sum_xl,
        back_matmul, back_to_z, pre_grad, grads_to_core, encoder_grads,
    )
    order = sorted(
        (STAGE_TIMES[j] + CHUNK_STEP * k, k, j) for k in range(chunks) for j in range(len(stages))
    )
    for _, k, j in order:
        stages[j](k)
        if (k, j) == (chunks - 1, 8):
            decoder_grads()

    for i, ref in pending:
        wait(0, i, ref)


def step(residual, norm_gain, gate_weight, up_weight, down_weight, encoder, encoder_bias, decoder, width):
    layers, local, cols = residual.shape
    feats = encoder.shape[1]
    hid = gate_weight.shape[2]
    chunks, slots, rows = 3, 8, 16
    tokens = slots * rows
    both, wide = layers * feats, layers * cols
    gu_cols = -(-layers * hid // 128) * 128 + layers * hid
    vm = pltpu.VMEM
    scratch = [
        vm((8, layers, 8, 128), F32),
        vm((16, wide), F32),
        vm((8, 16, wide), BF16),
        vm((8 * local, wide), F32),
        vm((chunks, slots, rows, wide), BF16),
        vm((both + layers * hid, wide), BF16),
        vm((both, wide), BF16),
        vm((wide, gu_cols), BF16),
        vm((chunks, slots, rows, both), F32),
        vm((chunks, 4, rows, both), F32),
        vm((chunks, 4, rows, both), F32),
        vm((chunks, 4, rows, both), F32),
        vm((chunks, slots, rows, gu_cols), BF16),
        vm((chunks, 4, rows, gu_cols), BF16),
        vm((chunks, 4, rows, gu_cols), BF16),
        vm((chunks, 4, rows, gu_cols), BF16),
        vm((chunks, slots, rows, both + layers * hid), BF16),
        vm((chunks, slots, rows, wide), BF16),
        vm((chunks, slots, rows, wide), BF16),
        vm((chunks, 8, rows, wide), BF16),
        vm((chunks, slots, rows, wide), BF16),
        vm((chunks, both // slots, tokens), F32),
        vm((chunks, slots, both // slots, tokens), BF16),
        vm((chunks, 4, both // slots, tokens), BF16),
        vm((chunks, 4, both // slots, tokens), BF16),
        vm((chunks, 4, both // slots, tokens), BF16),
        vm((chunks, slots, both // slots, tokens), BF16),
        vm((layers, feats, cols), F32),
        pltpu.SemaphoreType.DMA((2, 2 + chunks * 14)),
    ]
    spec = pl.BlockSpec(memory_space=pltpu.VMEM)
    return pl.pallas_call(
        functools.partial(kernel, width),
        out_shape=(
            jax.ShapeDtypeStruct(encoder.shape, BF16),
            jax.ShapeDtypeStruct(encoder_bias.shape, F32),
            jax.ShapeDtypeStruct(decoder.shape, BF16),
        ),
        in_specs=[spec] * 8,
        out_specs=(spec,) * 3,
        scratch_shapes=scratch,
        compiler_params=pltpu.CompilerParams(
            collective_id=0, has_side_effects=True, vmem_limit_bytes=56 * 2**20
        ),
        name="train_step",
    )(residual, norm_gain, gate_weight, up_weight, down_weight, encoder, encoder_bias, decoder)


def solution(mesh):
    def body(*args):
        return step(*args, width=args[0].shape[2] * mesh.shape["mp"])

    return jax.shard_map(
        body,
        mesh=mesh,
        in_specs=(
            P(None, "feat", "mp"),
            P(None, "mp"),
            P(None, "mp", "feat"),
            P(None, "mp", "feat"),
            P(None, "feat", "mp"),
            P(None, "feat", "mp"),
            P(None, "feat"),
            P(None, "feat", "mp"),
        ),
        out_specs=(P(None, "feat", "mp"), P(None, "feat"), P(None, "feat", "mp")),
        check_vma=False,
    )
```

```python
import functools
import math

import jax
import jax.numpy as jnp
from jax import lax
from jax.experimental import pallas as pl
from jax.experimental.pallas import tpu as pltpu
from jax.sharding import PartitionSpec as P

MESH = pl.DeviceIdType.MESH
F32 = jnp.float32
BF16 = jnp.bfloat16
sparsity_weight = 0.1

ROWS = (16, 16, 16)
STAGE_TIMES = (0, 1.5, 9, 14, 16, 21, 27, 31, 33, 38, 43, 45)
CHUNK_STEP = 9.0


def nt(a, b):
    return lax.dot_general(a, b, (((1,), (1,)), ((), ())), preferred_element_type=F32)


def kernel(
    width, residual, gain, gate_hbm, up_hbm, down_hbm, encoder, bias, decoder,
    grad_encoder, grad_bias, grad_decoder,
    squares, padded, y_block, own_block, w_dec, w_enc, w_gate, w_down, gate_w, up_w, down_w,
    normed_t, errors_t, enc_sum, sems, local_sems, *per_chunk,
):
    layers, cols, feats = encoder.shape
    local = residual.shape[0]
    hid = gate_w.shape[1]
    chunks, slots = len(ROWS), 8
    both = layers * feats
    tokens = slots * sum(ROWS)
    chunk_tokens = [slots * rows for rows in ROWS]
    first_row = [sum(ROWS[:k]) for k in range(chunks)]
    first_token = [slots * row for row in first_row]
    (
        normed, pre_mine, pre_core, pre_z, pre_recv, gu_mine, gu_core, gu_z, gu_recv, act,
        hidden_all, err_part, err_recv, err_y, errors, back_mine, back_core, back_z, back_recv, grads,
    ) = [per_chunk[i : i + chunks] for i in range(0, len(per_chunk), chunks)]
    scale = 1.0 / math.sqrt(tokens)

    mp = lax.axis_index("mp")
    ft = lax.axis_index("feat")
    zh, core = mp // 2, mp % 2
    xl, yy = ft // 8, ft % 8
    mine = core * 4 + zh

    core_dev = (zh * 2 + 1 - core, ft)
    z_at = [(zh + d) % 4 for d in (1, 2, 3)]
    z_dev = [(z * 2 + core, ft) for z in z_at]
    far_dev = [(z * 2 + 1 - core, ft) for z in z_at]
    xl_at = [(xl + d) % 8 for d in range(1, 8)]
    xl_dev = [(mp, a * 8 + yy) for a in xl_at]
    y_at = [(yy + d) % 8 for d in range(1, 8)]
    y_dev = [(mp, xl * 8 + a) for a in y_at]
    partners = [core_dev] + z_dev + far_dev + xl_dev + y_dev

    pending = []

    def send(i, src, dst, dev):
        pltpu.make_async_remote_copy(
            src_ref=src, dst_ref=dst, send_sem=sems.at[0, i], recv_sem=sems.at[1, i],
            device_id=dev, device_id_type=MESH,
        ).start()

    def wait(side, i, ref):
        pltpu.make_async_copy(ref, ref, sems.at[side, i]).wait()

    barrier = pltpu.get_barrier_semaphore()
    for dev in partners:
        pl.semaphore_signal(barrier, inc=1, device_id=dev, device_id_type=MESH)

    copies = [
        pltpu.make_async_copy(src, dst, local_sems.at[i])
        for i, (src, dst) in enumerate((
            (encoder.at[0], w_enc.at[0:cols, 0:feats]),
            (encoder.at[1], w_enc.at[cols : 2 * cols, feats:both]),
            (decoder.at[0], w_dec.at[0:cols, 0:feats]),
            (decoder.at[1], w_dec.at[cols : 2 * cols, 0:feats]),
            (decoder.at[2], w_dec.at[cols : 2 * cols, feats:both]),
            (gate_hbm, gate_w),
            (up_hbm, up_w),
            (down_hbm, down_w),
        ))
    ]
    for copy in copies:
        copy.start()

    stacked = residual[...].astype(F32)
    values = [stacked[:, l, :] for l in range(layers)]
    sums = [jnp.sum(v * v, axis=1, keepdims=True) for v in values]
    lanes = lax.broadcasted_iota(jnp.int32, (local, 128), 1)
    squares[mp] = jnp.zeros((8, 128), F32)
    squares[mp, 0:local, :] = jnp.where(lanes < 64, sums[0], sums[1])
    padded[...] = jnp.zeros_like(padded)

    pl.semaphore_wait(barrier, len(partners))

    for dev in z_dev + far_dev + [core_dev]:
        send(0, squares.at[mp], squares.at[mp], dev)
    pending.append((0, squares.at[0:7]))

    w_enc[0:cols, feats:both] = jnp.zeros((cols, feats), BF16)
    w_enc[cols : 2 * cols, 0:feats] = jnp.zeros((cols, feats), BF16)
    w_dec[0:cols, feats:both] = jnp.zeros((cols, feats), BF16)
    up_at = 2 * hid
    w_gate[...] = jnp.zeros_like(w_gate)
    w_down[...] = jnp.zeros_like(w_down)

    wait(1, 0, squares.at[0:7])
    total = squares[0]
    for m in range(1, 8):
        total = total + squares[m]
    for l in range(layers):
        inverse = lax.rsqrt(total[0:local, 64 * l : 64 * l + 1] / width + 1e-06)
        padded[l * local : (l + 1) * local, :] = values[l] * inverse * gain[l : l + 1, :]
    y_block[yy] = padded[...].astype(BF16)
    for dev in y_dev:
        send(1, y_block.at[yy], y_block.at[yy], dev)
    pending.append((1, y_block.at[0:7]))

    for copy in copies:
        copy.wait()
    for l in range(layers):
        d, h = slice(l * cols, (l + 1) * cols), slice(l * hid, (l + 1) * hid)
        w_gate[h, d] = gate_w[l]
        w_gate[up_at + l * hid : up_at + (l + 1) * hid, d] = up_w[l]
        w_down[h, d] = down_w[l]

    wait(1, 1, y_block.at[0:7])
    for s in range(8):
        arrived = y_block[s].astype(F32)
        for l in range(layers):
            own_block[s * local : (s + 1) * local, l * cols : (l + 1) * cols] = arrived[
                l * local : (l + 1) * local, :
            ]
    for k in range(chunks):
        normed[k][xl] = own_block[first_row[k] : first_row[k] + ROWS[k], :].astype(BF16)
        for dev in xl_dev:
            send(2 + k, normed[k].at[xl], normed[k].at[xl], dev)
        pending.append((2 + k, normed[k].at[0:7]))

    def slot(kind, k):
        return 2 + chunks * (1 + kind) + k

    def pre_matmul(k):
        wait(1, 2 + k, normed[k].at[0:7])
        x = normed[k][...].reshape(chunk_tokens[k], 2 * cols)
        pre_mine[k][...] = jnp.dot(x, w_enc[...], preferred_element_type=F32).reshape(slots, ROWS[k], both)
        send(slot(0, k), pre_mine[k].at[pl.ds((1 - core) * 4, 4)], pre_core[k], core_dev)
        pending.append((slot(0, k), pre_core[k]))
        gu_mine[k][...] = nt(x, w_gate[...]).astype(BF16).reshape(slots, ROWS[k], -1)
        send(slot(1, k), gu_mine[k].at[pl.ds((1 - core) * 4, 4)], gu_core[k], core_dev)
        pending.append((slot(1, k), gu_core[k]))

    def pre_to_z(k):
        wait(1, slot(0, k), pre_core[k])
        for z, dev in zip(z_at, z_dev):
            pre_z[k][z] = pre_mine[k][core * 4 + z] + pre_core[k][z]
            send(slot(2, k), pre_z[k].at[z], pre_recv[k].at[zh], dev)
        pending.append((slot(2, k), pre_z[k].at[0:3]))
        pre_recv[k][zh] = pre_mine[k][mine] + pre_core[k][zh]
        wait(1, slot(1, k), gu_core[k])
        for z, dev in zip(z_at, z_dev):
            gu_z[k][z] = (gu_mine[k][core * 4 + z].astype(F32) + gu_core[k][z].astype(F32)).astype(BF16)
            send(slot(3, k), gu_z[k].at[z], gu_recv[k].at[zh], dev)
        pending.append((slot(3, k), gu_z[k].at[0:3]))
        gu_recv[k][zh] = (gu_mine[k][mine].astype(F32) + gu_core[k][zh].astype(F32)).astype(BF16)
        normed_t[:, first_token[k] : first_token[k] + chunk_tokens[k]] = normed[k][...].reshape(chunk_tokens[k], 2 * cols).T

    def activate(k):
        wait(1, slot(2, k), pre_recv[k].at[0:3])
        total = pre_recv[k][0] + pre_recv[k][1] + pre_recv[k][2] + pre_recv[k][3]
        for l in range(layers):
            act[k][mine, :, l * feats : (l + 1) * feats] = jnp.maximum(
                total[:, l * feats : (l + 1) * feats] + bias[l : l + 1, :], 0.0
            ).astype(BF16)
        for dev in z_dev:
            send(slot(4, k), act[k].at[mine], act[k].at[mine], dev)
        pending.append((slot(4, k), act[k].at[0:3]))
        wait(1, slot(3, k), gu_recv[k].at[0:3])
        gu = gu_recv[k][0].astype(F32)
        for z in range(1, 4):
            gu = gu + gu_recv[k][z].astype(F32)
        hidden = jax.nn.gelu(gu[:, 0 : 2 * hid], approximate=True) * gu[:, up_at : up_at + 2 * hid]
        hidden_all[k][mine] = hidden.astype(BF16)
        for dev in z_dev:
            send(slot(13, k), hidden_all[k].at[mine], hidden_all[k].at[mine], dev)
        pending.append((slot(13, k), hidden_all[k].at[0:3]))

    def act_to_core(k):
        wait(1, slot(4, k), act[k].at[0:3])
        half = act[k].at[pl.ds(core * 4, 4)]
        send(slot(5, k), half, half, core_dev)
        pending.append((slot(5, k), act[k].at[0:4]))
        wait(1, slot(13, k), hidden_all[k].at[0:3])
        half = hidden_all[k].at[pl.ds(core * 4, 4)]
        send(slot(14, k), half, half, core_dev)
        pending.append((slot(14, k), hidden_all[k].at[0:4]))

    def rebuild(k):
        wait(1, slot(5, k), act[k].at[0:4])
        wait(1, slot(14, k), hidden_all[k].at[0:4])
        part = nt(act[k][...].reshape(chunk_tokens[k], both), w_dec[...]) - jnp.dot(
            hidden_all[k][...].reshape(chunk_tokens[k], 2 * hid), w_down[...], preferred_element_type=F32
        )
        err_part[k][...] = part.astype(BF16).reshape(slots, ROWS[k], -1)
        for s, dev in zip(xl_at, xl_dev):
            send(slot(6, k), err_part[k].at[s], err_recv[k].at[xl], dev)
        pending.append((slot(6, k), err_part[k].at[0:7]))
        err_recv[k][xl] = err_part[k][xl]

    def sum_first(k):
        wait(1, slot(6, k), err_recv[k].at[0:7])
        total = err_recv[k][0].astype(F32)
        for s in range(1, 8):
            total = total + err_recv[k][s].astype(F32)
        err_y[k][yy] = total.astype(BF16)
        for dev in y_dev:
            send(slot(7, k), err_y[k].at[yy], err_y[k].at[yy], dev)
        pending.append((slot(7, k), err_y[k].at[0:7]))

    def sum_y(k):
        wait(1, slot(7, k), err_y[k].at[0:7])
        total = err_y[k][0].astype(F32)
        for s in range(1, 8):
            total = total + err_y[k][s].astype(F32)
        errors[k][xl] = total.astype(BF16)
        for dev in xl_dev:
            send(slot(8, k), errors[k].at[xl], errors[k].at[xl], dev)
        pending.append((slot(8, k), errors[k].at[0:7]))

    def back_matmul(k):
        wait(1, slot(8, k), errors[k].at[0:7])
        e = errors[k][...].reshape(chunk_tokens[k], 2 * cols)
        back = jnp.dot(e, w_dec[...], preferred_element_type=F32)
        back_mine[k][...] = back.astype(BF16).reshape(slots, ROWS[k], both)
        send(slot(9, k), back_mine[k].at[pl.ds((1 - core) * 4, 4)], back_core[k], core_dev)
        pending.append((slot(9, k), back_core[k]))

    def back_to_z(k):
        wait(1, slot(9, k), back_core[k])
        for z, dev in zip(z_at, z_dev):
            back_z[k][z] = (
                back_mine[k][core * 4 + z].astype(F32) + back_core[k][z].astype(F32)
            ).astype(BF16)
            send(slot(10, k), back_z[k].at[z], back_recv[k].at[zh], dev)
        pending.append((slot(10, k), back_z[k].at[0:3]))
        back_recv[k][zh] = (
            back_mine[k][mine].astype(F32) + back_core[k][zh].astype(F32)
        ).astype(BF16)
        errors_t[:, first_token[k] : first_token[k] + chunk_tokens[k]] = errors[k][...].reshape(chunk_tokens[k], 2 * cols).T

    def pre_grad(k):
        wait(1, slot(10, k), back_recv[k].at[0:3])
        total = back_recv[k][0].astype(F32)
        for z in range(1, 4):
            total = total + back_recv[k][z].astype(F32)
        grads[k][mine] = jnp.where(
            act[k][mine].astype(F32) > 0, scale * (total + sparsity_weight), 0.0
        ).astype(BF16)
        for dev in z_dev:
            send(slot(11, k), grads[k].at[mine], grads[k].at[mine], dev)
        pending.append((slot(11, k), grads[k].at[0:3]))

    def grads_to_core(k):
        wait(1, slot(11, k), grads[k].at[0:3])
        half = grads[k].at[pl.ds(core * 4, 4)]
        send(slot(12, k), half, half, core_dev)
        pending.append((slot(12, k), grads[k].at[0:4]))

    def encoder_grads(k):
        wait(1, slot(12, k), grads[k].at[0:4])
        g = grads[k][...].reshape(chunk_tokens[k], both)
        ones = jnp.ones((8, chunk_tokens[k]), BF16)
        for l in range(layers):
            g_layer = g[:, l * feats : (l + 1) * feats]
            x_t = normed_t[l * cols : (l + 1) * cols, first_token[k] : first_token[k] + chunk_tokens[k]]
            part = jnp.dot(x_t, g_layer, preferred_element_type=F32)
            if k > 0:
                part = part + enc_sum[l]
            if k < chunks - 1:
                enc_sum[l] = part
            else:
                grad_encoder[l] = part.astype(BF16)
            column = jnp.dot(ones, g_layer, preferred_element_type=F32)[0:1]
            if k > 0:
                column = column + grad_bias[l : l + 1, :]
            grad_bias[l : l + 1, :] = column

    def decoder_grads():
        first = second = None
        for k in range(chunks):
            a = act[k][...].reshape(chunk_tokens[k], both)
            e = errors_t[:, first_token[k] : first_token[k] + chunk_tokens[k]]
            one = jnp.dot(e, a[:, 0:feats], preferred_element_type=F32)
            two = jnp.dot(e[cols : 2 * cols], a[:, feats:both], preferred_element_type=F32)
            first, second = (one, two) if k == 0 else (first + one, second + two)
        grad_decoder[0] = (first[0:cols] * scale).astype(BF16)
        grad_decoder[1] = (first[cols : 2 * cols] * scale).astype(BF16)
        grad_decoder[2] = (second * scale).astype(BF16)

    stages = (
        pre_matmul, pre_to_z, activate, act_to_core, rebuild, sum_first, sum_y,
        back_matmul, back_to_z, pre_grad, grads_to_core, encoder_grads,
    )
    order = sorted(
        (STAGE_TIMES[j] + CHUNK_STEP * k, k, j) for k in range(chunks) for j in range(len(stages))
    )
    for _, k, j in order:
        stages[j](k)
        if (k, j) == (chunks - 1, 8):
            decoder_grads()

    for i, ref in pending:
        wait(0, i, ref)


def step(residual, norm_gain, gate_weight, up_weight, down_weight, encoder, encoder_bias, decoder, width):
    layers, local, cols = residual.shape
    feats = encoder.shape[1]
    hid = gate_weight.shape[2]
    chunks, slots = len(ROWS), 8
    tokens = slots * sum(ROWS)
    both, wide, hidden, gate_up = layers * feats, layers * cols, layers * hid, 2 * layers * hid
    vm = pltpu.VMEM
    scratch = [
        vm((8, 8, 128), F32),
        vm((16, cols), F32),
        vm((8, 16, cols), BF16),
        vm((8 * local, wide), F32),
        vm((wide, both), BF16),
        vm((wide, both), BF16),
        vm((gate_up, wide), BF16),
        vm((hidden, wide), BF16),
        vm((layers, hid, cols), BF16),
        vm((layers, hid, cols), BF16),
        vm((layers, hid, cols), BF16),
        vm((wide, tokens), BF16),
        vm((wide, tokens), BF16),
        vm((layers, cols, feats), F32),
        pltpu.SemaphoreType.DMA((2, 2 + chunks * 16)),
        pltpu.SemaphoreType.DMA((8,)),
    ]
    for lead, last, dtype in (
        (slots, wide, BF16),
        (slots, both, F32), (4, both, F32), (4, both, F32), (4, both, F32),
        (slots, gate_up, BF16), (4, gate_up, BF16), (4, gate_up, BF16), (4, gate_up, BF16),
        (slots, both, BF16), (slots, hidden, BF16),
        (slots, wide, BF16), (slots, wide, BF16), (8, wide, BF16), (slots, wide, BF16),
        (slots, both, BF16), (4, both, BF16), (4, both, BF16), (4, both, BF16), (slots, both, BF16),
    ):
        scratch += [vm((lead, rows, last), dtype) for rows in ROWS]
    spec = pl.BlockSpec(memory_space=pltpu.VMEM)
    anywhere = pl.BlockSpec(memory_space=pl.ANY)
    grad_encoder, grad_bias, grad_decoder = pl.pallas_call(
        functools.partial(kernel, width),
        out_shape=(
            jax.ShapeDtypeStruct((layers, cols, feats), BF16),
            jax.ShapeDtypeStruct(encoder_bias.shape, F32),
            jax.ShapeDtypeStruct((decoder.shape[0], cols, feats), BF16),
        ),
        in_specs=[spec, spec, anywhere, anywhere, anywhere, anywhere, spec, anywhere],
        out_specs=(spec,) * 3,
        scratch_shapes=scratch,
        compiler_params=pltpu.CompilerParams(
            collective_id=0, has_side_effects=True, vmem_limit_bytes=56 * 2**20
        ),
        name="train_step",
    )(
        residual.swapaxes(0, 1), norm_gain, gate_weight.swapaxes(1, 2), up_weight.swapaxes(1, 2),
        down_weight, encoder.swapaxes(1, 2), encoder_bias, decoder.swapaxes(1, 2),
    )
    return grad_encoder.swapaxes(1, 2), grad_bias, grad_decoder.swapaxes(1, 2)


def solution(mesh):
    def body(*args):
        return step(*args, width=args[0].shape[2] * mesh.shape["mp"])

    return jax.shard_map(
        body,
        mesh=mesh,
        in_specs=(
            P(None, "feat", "mp"),
            P(None, "mp"),
            P(None, "mp", "feat"),
            P(None, "mp", "feat"),
            P(None, "feat", "mp"),
            P(None, "feat", "mp"),
            P(None, "feat"),
            P(None, "feat", "mp"),
        ),
        out_specs=(P(None, "feat", "mp"), P(None, "feat"), P(None, "feat", "mp")),
        check_vma=False,
    )
```

```python
import functools
import math

import jax
import jax.numpy as jnp
from jax import lax
from jax.experimental import pallas as pl
from jax.experimental.pallas import tpu as pltpu
from jax.sharding import PartitionSpec as P

MESH = pl.DeviceIdType.MESH
F32 = jnp.float32
BF16 = jnp.bfloat16
sparsity_weight = 0.1

ROWS = (16, 16, 16)
STAGE_TIMES = (0, 1.5, 9, 14, 16, 21, 27, 31, 33, 38, 43, 45)
CHUNK_STEP = 9.0


def nt(a, b):
    return lax.dot_general(a, b, (((1,), (1,)), ((), ())), preferred_element_type=F32)


def kernel(
    width, residual, gain, gate_hbm, up_hbm, down_hbm, encoder, bias, decoder,
    grad_encoder, grad_bias, grad_decoder,
    squares, padded, plane_block, own_block, w_dec, w_enc, w_gate, w_down, gate_w, up_w, down_w,
    normed_t, errors_t, enc_sum, sems, local_sems, *per_chunk,
):
    layers, cols, feats = encoder.shape
    local = residual.shape[0]
    hid = gate_w.shape[1]
    chunks, slots = len(ROWS), 8
    both = layers * feats
    tokens = slots * sum(ROWS)
    chunk_tokens = [slots * rows for rows in ROWS]
    first_row = [sum(ROWS[:k]) for k in range(chunks)]
    first_token = [slots * row for row in first_row]
    (
        normed, pre_mine, pre_core, pre_z, pre_recv, gu_mine, gu_core, gu_z, gu_recv, act,
        hidden_all, err_part, err_recv, err_y, errors, back_mine, back_core, back_z, back_recv, grads,
    ) = [per_chunk[i : i + chunks] for i in range(0, len(per_chunk), chunks)]
    scale = 1.0 / math.sqrt(tokens)

    mp = lax.axis_index("mp")
    ft = lax.axis_index("feat")
    zh, core = mp // 2, mp % 2
    xl, yy = ft // 8, ft % 8
    xx, plane = xl % 4, xl // 4 * 8 + yy
    mine = core * 4 + zh

    core_dev = (zh * 2 + 1 - core, ft)
    z_at = [(zh + d) % 4 for d in (2, 1, 3)]
    z_dev = [(z * 2 + core, ft) for z in z_at]
    far_dev = [(z * 2 + 1 - core, ft) for z in z_at]
    xl_at = [(xl + d) % 8 for d in range(1, 8)]
    xl_dev = [(mp, a * 8 + yy) for a in xl_at]
    x_dev = [(mp, (xl // 4 * 4 + (xx + d) % 4) * 8 + yy) for d in (2, 1, 3)]
    y_dev = [(mp, xl * 8 + (yy + d) % 8) for d in (4, 3, 5, 2, 6, 1, 7)]
    plane_at = [(plane + d) % 16 for d in range(1, 16)]
    plane_dev = [(mp, (a // 8 * 4 + xx) * 8 + a % 8) for a in plane_at]
    diagonal_dev = [(mp, ((1 - xl // 4) * 4 + (xx + d) % 4) * 8 + yy) for d in (1, 2, 3)]
    partners = [core_dev] + z_dev + far_dev + x_dev + diagonal_dev + plane_dev

    pending = []

    def send(i, src, dst, dev):
        pltpu.make_async_remote_copy(
            src_ref=src, dst_ref=dst, send_sem=sems.at[0, i], recv_sem=sems.at[1, i],
            device_id=dev, device_id_type=MESH,
        ).start()

    def wait(side, i, ref):
        pltpu.make_async_copy(ref, ref, sems.at[side, i]).wait()

    barrier = pltpu.get_barrier_semaphore()
    for dev in partners:
        pl.semaphore_signal(barrier, inc=1, device_id=dev, device_id_type=MESH)

    copies = [
        pltpu.make_async_copy(src, dst, local_sems.at[i])
        for i, (src, dst) in enumerate((
            (encoder.at[0], w_enc.at[0:cols, 0:feats]),
            (encoder.at[1], w_enc.at[cols : 2 * cols, feats:both]),
            (decoder.at[0], w_dec.at[0:cols, 0:feats]),
            (decoder.at[1], w_dec.at[cols : 2 * cols, 0:feats]),
            (decoder.at[2], w_dec.at[cols : 2 * cols, feats:both]),
            (gate_hbm, gate_w),
            (up_hbm, up_w),
            (down_hbm, down_w),
        ))
    ]
    for copy in copies:
        copy.start()

    stacked = residual[...].astype(F32)
    values = [stacked[:, l, :] for l in range(layers)]
    sums = [jnp.sum(v * v, axis=1, keepdims=True) for v in values]
    lanes = lax.broadcasted_iota(jnp.int32, (local, 128), 1)
    squares[mp] = jnp.zeros((8, 128), F32)
    squares[mp, 0:local, :] = jnp.where(lanes < 64, sums[0], sums[1])
    padded[...] = jnp.zeros_like(padded)

    pl.semaphore_wait(barrier, len(partners))

    for dev in z_dev + far_dev + [core_dev]:
        send(0, squares.at[mp], squares.at[mp], dev)
    pending.append((0, squares.at[0:7]))

    w_enc[0:cols, feats:both] = jnp.zeros((cols, feats), BF16)
    w_enc[cols : 2 * cols, 0:feats] = jnp.zeros((cols, feats), BF16)
    w_dec[0:cols, feats:both] = jnp.zeros((cols, feats), BF16)
    up_at = 2 * hid
    w_gate[...] = jnp.zeros_like(w_gate)
    w_down[...] = jnp.zeros_like(w_down)

    wait(1, 0, squares.at[0:7])
    total = squares[0]
    for m in range(1, 8):
        total = total + squares[m]
    for l in range(layers):
        inverse = lax.rsqrt(total[0:local, 64 * l : 64 * l + 1] / width + 1e-06)
        padded[l * local : (l + 1) * local, :] = values[l] * inverse * gain[l : l + 1, :]
    plane_block[plane] = padded[...].astype(BF16)
    for dev in plane_dev:
        send(1, plane_block.at[plane], plane_block.at[plane], dev)
    pending.append((1, plane_block.at[0:15]))

    for copy in copies:
        copy.wait()
    for l in range(layers):
        d, h = slice(l * cols, (l + 1) * cols), slice(l * hid, (l + 1) * hid)
        w_gate[h, d] = gate_w[l]
        w_gate[up_at + l * hid : up_at + (l + 1) * hid, d] = up_w[l]
        w_down[h, d] = down_w[l]

    wait(1, 1, plane_block.at[0:15])
    for s in range(16):
        arrived = plane_block[s].astype(F32)
        for l in range(layers):
            own_block[s * local : (s + 1) * local, l * cols : (l + 1) * cols] = arrived[
                l * local : (l + 1) * local, :
            ]
    for k in range(chunks):
        normed[k][xx] = own_block[2 * first_row[k] : 2 * (first_row[k] + ROWS[k]), :].astype(BF16)
        for dev in x_dev:
            send(2 + k, normed[k].at[xx], normed[k].at[xx], dev)
        pending.append((2 + k, normed[k].at[0:3]))

    def slot(kind, k):
        return 2 + chunks * (1 + kind) + k

    def pre_matmul(k):
        wait(1, 2 + k, normed[k].at[0:3])
        x = normed[k][...].reshape(chunk_tokens[k], 2 * cols)
        pre_mine[k][...] = jnp.dot(x, w_enc[...], preferred_element_type=F32).reshape(slots, ROWS[k], both)
        send(slot(0, k), pre_mine[k].at[pl.ds((1 - core) * 4, 4)], pre_core[k], core_dev)
        pending.append((slot(0, k), pre_core[k]))
        gu_mine[k][...] = nt(x, w_gate[...]).astype(BF16).reshape(slots, ROWS[k], -1)
        send(slot(1, k), gu_mine[k].at[pl.ds((1 - core) * 4, 4)], gu_core[k], core_dev)
        pending.append((slot(1, k), gu_core[k]))

    def pre_to_z(k):
        wait(1, slot(0, k), pre_core[k])
        for z, dev in zip(z_at, z_dev):
            pre_z[k][z] = pre_mine[k][core * 4 + z] + pre_core[k][z]
            send(slot(2, k), pre_z[k].at[z], pre_recv[k].at[zh], dev)
        pending.append((slot(2, k), pre_z[k].at[0:3]))
        pre_recv[k][zh] = pre_mine[k][mine] + pre_core[k][zh]
        wait(1, slot(1, k), gu_core[k])
        for z, dev in zip(z_at, z_dev):
            gu_z[k][z] = (gu_mine[k][core * 4 + z].astype(F32) + gu_core[k][z].astype(F32)).astype(BF16)
            send(slot(3, k), gu_z[k].at[z], gu_recv[k].at[zh], dev)
        pending.append((slot(3, k), gu_z[k].at[0:3]))
        gu_recv[k][zh] = (gu_mine[k][mine].astype(F32) + gu_core[k][zh].astype(F32)).astype(BF16)
        normed_t[:, first_token[k] : first_token[k] + chunk_tokens[k]] = normed[k][...].reshape(chunk_tokens[k], 2 * cols).T

    def activate(k):
        wait(1, slot(2, k), pre_recv[k].at[0:3])
        total = pre_recv[k][0] + pre_recv[k][1] + pre_recv[k][2] + pre_recv[k][3]
        for l in range(layers):
            act[k][mine, :, l * feats : (l + 1) * feats] = jnp.maximum(
                total[:, l * feats : (l + 1) * feats] + bias[l : l + 1, :], 0.0
            ).astype(BF16)
        for dev in z_dev:
            send(slot(4, k), act[k].at[mine], act[k].at[mine], dev)
        pending.append((slot(4, k), act[k].at[0:3]))
        wait(1, slot(3, k), gu_recv[k].at[0:3])
        gu = gu_recv[k][0].astype(F32)
        for z in range(1, 4):
            gu = gu + gu_recv[k][z].astype(F32)
        hidden = jax.nn.gelu(gu[:, 0 : 2 * hid], approximate=True) * gu[:, up_at : up_at + 2 * hid]
        hidden_all[k][mine] = hidden.astype(BF16)
        for dev in z_dev:
            send(slot(13, k), hidden_all[k].at[mine], hidden_all[k].at[mine], dev)
        pending.append((slot(13, k), hidden_all[k].at[0:3]))

    def act_to_core(k):
        wait(1, slot(4, k), act[k].at[0:3])
        half = act[k].at[pl.ds(core * 4, 4)]
        send(slot(5, k), half, half, core_dev)
        pending.append((slot(5, k), act[k].at[0:4]))
        wait(1, slot(13, k), hidden_all[k].at[0:3])
        half = hidden_all[k].at[pl.ds(core * 4, 4)]
        send(slot(14, k), half, half, core_dev)
        pending.append((slot(14, k), hidden_all[k].at[0:4]))

    def rebuild(k):
        wait(1, slot(5, k), act[k].at[0:4])
        wait(1, slot(14, k), hidden_all[k].at[0:4])
        part = nt(act[k][...].reshape(chunk_tokens[k], both), w_dec[...]) - jnp.dot(
            hidden_all[k][...].reshape(chunk_tokens[k], 2 * hid), w_down[...], preferred_element_type=F32
        )
        err_part[k][...] = part.astype(BF16).reshape(slots, ROWS[k], -1)
        for s, dev in zip(xl_at, xl_dev):
            send(slot(6, k), err_part[k].at[s], err_recv[k].at[xl], dev)
        pending.append((slot(6, k), err_part[k].at[0:7]))
        err_recv[k][xl] = err_part[k][xl]

    def sum_first(k):
        wait(1, slot(6, k), err_recv[k].at[0:7])
        total = err_recv[k][0].astype(F32)
        for s in range(1, 8):
            total = total + err_recv[k][s].astype(F32)
        err_y[k][yy] = total.astype(BF16)
        for dev in y_dev:
            send(slot(7, k), err_y[k].at[yy], err_y[k].at[yy], dev)
        pending.append((slot(7, k), err_y[k].at[0:7]))

    def sum_y(k):
        wait(1, slot(7, k), err_y[k].at[0:7])
        total = err_y[k][0].astype(F32)
        for s in range(1, 8):
            total = total + err_y[k][s].astype(F32)
        errors[k][xl] = total.astype(BF16)
        for dev in xl_dev:
            send(slot(8, k), errors[k].at[xl], errors[k].at[xl], dev)
        pending.append((slot(8, k), errors[k].at[0:7]))

    def back_matmul(k):
        wait(1, slot(8, k), errors[k].at[0:7])
        e = errors[k][...].reshape(chunk_tokens[k], 2 * cols)
        back = jnp.dot(e, w_dec[...], preferred_element_type=F32)
        back_mine[k][...] = back.astype(BF16).reshape(slots, ROWS[k], both)
        send(slot(9, k), back_mine[k].at[pl.ds((1 - core) * 4, 4)], back_core[k], core_dev)
        pending.append((slot(9, k), back_core[k]))

    def back_to_z(k):
        wait(1, slot(9, k), back_core[k])
        for z, dev in zip(z_at, z_dev):
            back_z[k][z] = (
                back_mine[k][core * 4 + z].astype(F32) + back_core[k][z].astype(F32)
            ).astype(BF16)
            send(slot(10, k), back_z[k].at[z], back_recv[k].at[zh], dev)
        pending.append((slot(10, k), back_z[k].at[0:3]))
        back_recv[k][zh] = (
            back_mine[k][mine].astype(F32) + back_core[k][zh].astype(F32)
        ).astype(BF16)
        errors_t[:, first_token[k] : first_token[k] + chunk_tokens[k]] = errors[k][...].reshape(chunk_tokens[k], 2 * cols).T

    def pre_grad(k):
        wait(1, slot(10, k), back_recv[k].at[0:3])
        total = back_recv[k][0].astype(F32)
        for z in range(1, 4):
            total = total + back_recv[k][z].astype(F32)
        grads[k][mine] = jnp.where(
            act[k][mine].astype(F32) > 0, scale * (total + sparsity_weight), 0.0
        ).astype(BF16)
        for dev in z_dev:
            send(slot(11, k), grads[k].at[mine], grads[k].at[mine], dev)
        pending.append((slot(11, k), grads[k].at[0:3]))

    def grads_to_core(k):
        wait(1, slot(11, k), grads[k].at[0:3])
        half = grads[k].at[pl.ds(core * 4, 4)]
        send(slot(12, k), half, half, core_dev)
        pending.append((slot(12, k), grads[k].at[0:4]))

    def encoder_grads(k):
        wait(1, slot(12, k), grads[k].at[0:4])
        g = grads[k][...].reshape(chunk_tokens[k], both)
        ones = jnp.ones((8, chunk_tokens[k]), BF16)
        for l in range(layers):
            g_layer = g[:, l * feats : (l + 1) * feats]
            x_t = normed_t[l * cols : (l + 1) * cols, first_token[k] : first_token[k] + chunk_tokens[k]]
            part = jnp.dot(x_t, g_layer, preferred_element_type=F32)
            if k > 0:
                part = part + enc_sum[l]
            if k < chunks - 1:
                enc_sum[l] = part
            else:
                grad_encoder[l] = part.astype(BF16)
            column = jnp.dot(ones, g_layer, preferred_element_type=F32)[0:1]
            if k > 0:
                column = column + grad_bias[l : l + 1, :]
            grad_bias[l : l + 1, :] = column

    def decoder_grads():
        first = second = None
        for k in range(chunks):
            a = act[k][...].reshape(chunk_tokens[k], both)
            e = errors_t[:, first_token[k] : first_token[k] + chunk_tokens[k]]
            one = jnp.dot(e, a[:, 0:feats], preferred_element_type=F32)
            two = jnp.dot(e[cols : 2 * cols], a[:, feats:both], preferred_element_type=F32)
            first, second = (one, two) if k == 0 else (first + one, second + two)
        grad_decoder[0] = (first[0:cols] * scale).astype(BF16)
        grad_decoder[1] = (first[cols : 2 * cols] * scale).astype(BF16)
        grad_decoder[2] = (second * scale).astype(BF16)

    stages = (
        pre_matmul, pre_to_z, activate, act_to_core, rebuild, sum_first, sum_y,
        back_matmul, back_to_z, pre_grad, grads_to_core, encoder_grads,
    )
    order = sorted(
        (STAGE_TIMES[j] + CHUNK_STEP * k, k, j) for k in range(chunks) for j in range(len(stages))
    )
    for _, k, j in order:
        stages[j](k)
        if (k, j) == (chunks - 1, 8):
            decoder_grads()

    for i, ref in pending:
        wait(0, i, ref)


def hand_over(*refs):
    copies = [
        pltpu.make_async_copy(refs[i], refs[3 + i], refs[6].at[i]) for i in range(3)
    ]
    for copy in copies:
        copy.start()
    for copy in copies:
        copy.wait()


def step(residual, norm_gain, gate_weight, up_weight, down_weight, encoder, encoder_bias, decoder, width):
    layers, local, cols = residual.shape
    feats = encoder.shape[1]
    hid = gate_weight.shape[2]
    chunks, slots = len(ROWS), 8
    tokens = slots * sum(ROWS)
    both, wide, hidden, gate_up = layers * feats, layers * cols, layers * hid, 2 * layers * hid
    vm = pltpu.VMEM
    scratch = [
        vm((8, 8, 128), F32),
        vm((16, cols), F32),
        vm((16, 16, cols), BF16),
        vm((16 * local, wide), F32),
        vm((wide, both), BF16),
        vm((wide, both), BF16),
        vm((gate_up, wide), BF16),
        vm((hidden, wide), BF16),
        vm((layers, hid, cols), BF16),
        vm((layers, hid, cols), BF16),
        vm((layers, hid, cols), BF16),
        vm((wide, tokens), BF16),
        vm((wide, tokens), BF16),
        vm((layers, cols, feats), F32),
        pltpu.SemaphoreType.DMA((2, 2 + chunks * 16)),
        pltpu.SemaphoreType.DMA((8,)),
    ]
    scratch += [vm((4, 2 * rows, wide), BF16) for rows in ROWS]
    for lead, last, dtype in (
        (slots, both, F32), (4, both, F32), (4, both, F32), (4, both, F32),
        (slots, gate_up, BF16), (4, gate_up, BF16), (4, gate_up, BF16), (4, gate_up, BF16),
        (slots, both, BF16), (slots, hidden, BF16),
        (slots, wide, BF16), (slots, wide, BF16), (8, wide, BF16), (slots, wide, BF16),
        (slots, both, BF16), (4, both, BF16), (4, both, BF16), (4, both, BF16), (slots, both, BF16),
    ):
        scratch += [vm((lead, rows, last), dtype) for rows in ROWS]
    spec = pl.BlockSpec(memory_space=pltpu.VMEM)
    anywhere = pl.BlockSpec(memory_space=pl.ANY)
    grad_encoder, grad_bias, grad_decoder = pl.pallas_call(
        functools.partial(kernel, width),
        out_shape=(
            jax.ShapeDtypeStruct((layers, cols, feats), BF16),
            jax.ShapeDtypeStruct(encoder_bias.shape, F32),
            jax.ShapeDtypeStruct((decoder.shape[0], cols, feats), BF16),
        ),
        in_specs=[spec, spec, anywhere, anywhere, anywhere, anywhere, spec, anywhere],
        out_specs=(spec,) * 3,
        scratch_shapes=scratch,
        compiler_params=pltpu.CompilerParams(
            collective_id=0, has_side_effects=True, vmem_limit_bytes=56 * 2**20
        ),
        name="train_step",
    )(
        residual.swapaxes(0, 1), norm_gain, gate_weight.swapaxes(1, 2), up_weight.swapaxes(1, 2),
        down_weight, encoder.swapaxes(1, 2), encoder_bias, decoder.swapaxes(1, 2),
    )
    results = (grad_encoder, grad_bias, grad_decoder)
    grad_encoder, grad_bias, grad_decoder = pl.pallas_call(
        hand_over,
        out_shape=tuple(jax.ShapeDtypeStruct(r.shape, r.dtype) for r in results),
        in_specs=[anywhere] * 3,
        out_specs=(anywhere,) * 3,
        scratch_shapes=[pltpu.SemaphoreType.DMA((3,))],
        name="results",
    )(*results)
    return grad_encoder.swapaxes(1, 2), grad_bias, grad_decoder.swapaxes(1, 2)


def solution(mesh):
    def body(*args):
        return step(*args, width=args[0].shape[2] * mesh.shape["mp"])

    return jax.shard_map(
        body,
        mesh=mesh,
        in_specs=(
            P(None, "feat", "mp"),
            P(None, "mp"),
            P(None, "mp", "feat"),
            P(None, "mp", "feat"),
            P(None, "feat", "mp"),
            P(None, "feat", "mp"),
            P(None, "feat"),
            P(None, "feat", "mp"),
        ),
        out_specs=(P(None, "feat", "mp"), P(None, "feat"), P(None, "feat", "mp")),
        check_vma=False,
    )
```

```python
import functools
import math

import jax
import jax.numpy as jnp
from jax import lax
from jax.experimental import pallas as pl
from jax.experimental.pallas import tpu as pltpu
from jax.sharding import PartitionSpec as P

MESH = pl.DeviceIdType.MESH
F32 = jnp.float32
BF16 = jnp.bfloat16
sparsity_weight = 0.1

ROWS = (16, 16, 16)
STAGE_TIMES = (0, 1.5, 9, 14, 16, 21, 27, 31, 33, 38, 43, 45)
CHUNK_STEP = 9.0


def nt(a, b):
    return lax.dot_general(a, b, (((1,), (1,)), ((), ())), preferred_element_type=F32)


def kernel(
    width, residual, gain, gate_hbm, up_hbm, down_hbm, encoder, bias, decoder,
    grad_encoder, grad_bias, grad_decoder,
    squares, padded, plane_block, own_block, w_dec, w_enc, w_gate, w_down, gate_w, up_w, down_w,
    normed_t, errors_t, enc_sum, sems, local_sems, *per_chunk,
):
    layers, cols, feats = encoder.shape
    local = residual.shape[0]
    hid = gate_w.shape[1]
    chunks, slots = len(ROWS), 8
    both = layers * feats
    tokens = slots * sum(ROWS)
    chunk_tokens = [slots * rows for rows in ROWS]
    first_row = [sum(ROWS[:k]) for k in range(chunks)]
    first_token = [slots * row for row in first_row]
    (
        normed, pre_mine, pre_core, pre_z, pre_recv, gu_mine, gu_core, gu_z, gu_recv, act,
        hidden_all, err_part, err_recv, err_xl, errors, back_mine, back_core, back_z, back_recv, grads,
    ) = [per_chunk[i : i + chunks] for i in range(0, len(per_chunk), chunks)]
    scale = 1.0 / math.sqrt(tokens)

    mp = lax.axis_index("mp")
    ft = lax.axis_index("feat")
    zh, core = mp // 2, mp % 2
    xl, yy = ft // 8, ft % 8
    xx, plane = xl % 4, xl // 4 * 8 + yy
    mine = core * 4 + zh

    core_dev = (zh * 2 + 1 - core, ft)
    z_at = [(zh + d) % 4 for d in (2, 1, 3)]
    z_dev = [(z * 2 + core, ft) for z in z_at]
    far_dev = [(z * 2 + 1 - core, ft) for z in z_at]
    xl_at = [(xl + d) % 8 for d in range(1, 8)]
    xl_dev = [(mp, a * 8 + yy) for a in xl_at]
    x_dev = [(mp, (xl // 4 * 4 + (xx + d) % 4) * 8 + yy) for d in (2, 1, 3)]
    y_at = [(yy + d) % 8 for d in (4, 3, 5, 2, 6, 1, 7)]
    y_dev = [(mp, xl * 8 + a) for a in y_at]
    plane_at = [(plane + d) % 16 for d in range(1, 16)]
    plane_dev = [(mp, (a // 8 * 4 + xx) * 8 + a % 8) for a in plane_at]
    diagonal_dev = [(mp, ((1 - xl // 4) * 4 + (xx + d) % 4) * 8 + yy) for d in (1, 2, 3)]
    partners = [core_dev] + z_dev + far_dev + x_dev + diagonal_dev + plane_dev

    pending = []

    def send(i, src, dst, dev):
        pltpu.make_async_remote_copy(
            src_ref=src, dst_ref=dst, send_sem=sems.at[0, i], recv_sem=sems.at[1, i],
            device_id=dev, device_id_type=MESH,
        ).start()

    def wait(side, i, ref):
        pltpu.make_async_copy(ref, ref, sems.at[side, i]).wait()

    barrier = pltpu.get_barrier_semaphore()
    for dev in partners:
        pl.semaphore_signal(barrier, inc=1, device_id=dev, device_id_type=MESH)

    copies = [
        pltpu.make_async_copy(src, dst, local_sems.at[i])
        for i, (src, dst) in enumerate((
            (encoder.at[0], w_enc.at[0:cols, 0:feats]),
            (encoder.at[1], w_enc.at[cols : 2 * cols, feats:both]),
            (decoder.at[0], w_dec.at[0:cols, 0:feats]),
            (decoder.at[1], w_dec.at[cols : 2 * cols, 0:feats]),
            (decoder.at[2], w_dec.at[cols : 2 * cols, feats:both]),
            (gate_hbm, gate_w),
            (up_hbm, up_w),
            (down_hbm, down_w),
        ))
    ]
    for copy in copies:
        copy.start()

    stacked = residual[...].astype(F32)
    values = [stacked[:, l, :] for l in range(layers)]
    sums = [jnp.sum(v * v, axis=1, keepdims=True) for v in values]
    lanes = lax.broadcasted_iota(jnp.int32, (local, 128), 1)
    squares[mp] = jnp.zeros((8, 128), F32)
    squares[mp, 0:local, :] = jnp.where(lanes < 64, sums[0], sums[1])
    padded[...] = jnp.zeros_like(padded)

    pl.semaphore_wait(barrier, len(partners))

    for dev in z_dev + far_dev + [core_dev]:
        send(0, squares.at[mp], squares.at[mp], dev)
    pending.append((0, squares.at[0:7]))

    w_enc[0:cols, feats:both] = jnp.zeros((cols, feats), BF16)
    w_enc[cols : 2 * cols, 0:feats] = jnp.zeros((cols, feats), BF16)
    w_dec[0:cols, feats:both] = jnp.zeros((cols, feats), BF16)
    up_at = 2 * hid
    w_gate[...] = jnp.zeros_like(w_gate)
    w_down[...] = jnp.zeros_like(w_down)

    wait(1, 0, squares.at[0:7])
    total = squares[0]
    for m in range(1, 8):
        total = total + squares[m]
    for l in range(layers):
        inverse = lax.rsqrt(total[0:local, 64 * l : 64 * l + 1] / width + 1e-06)
        padded[l * local : (l + 1) * local, :] = values[l] * inverse * gain[l : l + 1, :]
    plane_block[plane] = padded[...].astype(BF16)
    for dev in plane_dev:
        send(1, plane_block.at[plane], plane_block.at[plane], dev)
    pending.append((1, plane_block.at[0:15]))

    for copy in copies:
        copy.wait()
    for l in range(layers):
        d, h = slice(l * cols, (l + 1) * cols), slice(l * hid, (l + 1) * hid)
        w_gate[h, d] = gate_w[l]
        w_gate[up_at + l * hid : up_at + (l + 1) * hid, d] = up_w[l]
        w_down[h, d] = down_w[l]

    wait(1, 1, plane_block.at[0:15])
    for s in range(16):
        arrived = plane_block[s].astype(F32)
        for l in range(layers):
            own_block[s * local : (s + 1) * local, l * cols : (l + 1) * cols] = arrived[
                l * local : (l + 1) * local, :
            ]
    for k in range(chunks):
        normed[k][xx] = own_block[2 * first_row[k] : 2 * (first_row[k] + ROWS[k]), :].astype(BF16)
        for dev in x_dev:
            send(2 + k, normed[k].at[xx], normed[k].at[xx], dev)
        pending.append((2 + k, normed[k].at[0:3]))

    def slot(kind, k):
        return 2 + chunks * (1 + kind) + k

    def pre_matmul(k):
        wait(1, 2 + k, normed[k].at[0:3])
        x = normed[k][...].reshape(chunk_tokens[k], 2 * cols)
        pre_mine[k][...] = jnp.dot(x, w_enc[...], preferred_element_type=F32).reshape(slots, ROWS[k], both)
        send(slot(0, k), pre_mine[k].at[pl.ds((1 - core) * 4, 4)], pre_core[k], core_dev)
        pending.append((slot(0, k), pre_core[k]))
        gu_mine[k][...] = nt(x, w_gate[...]).astype(BF16).reshape(slots, ROWS[k], -1)
        send(slot(1, k), gu_mine[k].at[pl.ds((1 - core) * 4, 4)], gu_core[k], core_dev)
        pending.append((slot(1, k), gu_core[k]))

    def pre_to_z(k):
        wait(1, slot(0, k), pre_core[k])
        for z, dev in zip(z_at, z_dev):
            pre_z[k][z] = pre_mine[k][core * 4 + z] + pre_core[k][z]
            send(slot(2, k), pre_z[k].at[z], pre_recv[k].at[zh], dev)
        pending.append((slot(2, k), pre_z[k].at[0:3]))
        pre_recv[k][zh] = pre_mine[k][mine] + pre_core[k][zh]
        wait(1, slot(1, k), gu_core[k])
        for z, dev in zip(z_at, z_dev):
            gu_z[k][z] = (gu_mine[k][core * 4 + z].astype(F32) + gu_core[k][z].astype(F32)).astype(BF16)
            send(slot(3, k), gu_z[k].at[z], gu_recv[k].at[zh], dev)
        pending.append((slot(3, k), gu_z[k].at[0:3]))
        gu_recv[k][zh] = (gu_mine[k][mine].astype(F32) + gu_core[k][zh].astype(F32)).astype(BF16)
        normed_t[:, first_token[k] : first_token[k] + chunk_tokens[k]] = normed[k][...].reshape(chunk_tokens[k], 2 * cols).T

    def activate(k):
        wait(1, slot(2, k), pre_recv[k].at[0:3])
        total = pre_recv[k][0] + pre_recv[k][1] + pre_recv[k][2] + pre_recv[k][3]
        for l in range(layers):
            act[k][mine, :, l * feats : (l + 1) * feats] = jnp.maximum(
                total[:, l * feats : (l + 1) * feats] + bias[l : l + 1, :], 0.0
            ).astype(BF16)
        for dev in z_dev:
            send(slot(4, k), act[k].at[mine], act[k].at[mine], dev)
        pending.append((slot(4, k), act[k].at[0:3]))
        wait(1, slot(3, k), gu_recv[k].at[0:3])
        gu = gu_recv[k][0].astype(F32)
        for z in range(1, 4):
            gu = gu + gu_recv[k][z].astype(F32)
        hidden = jax.nn.gelu(gu[:, 0 : 2 * hid], approximate=True) * gu[:, up_at : up_at + 2 * hid]
        hidden_all[k][mine] = hidden.astype(BF16)
        for dev in z_dev:
            send(slot(13, k), hidden_all[k].at[mine], hidden_all[k].at[mine], dev)
        pending.append((slot(13, k), hidden_all[k].at[0:3]))

    def act_to_core(k):
        wait(1, slot(4, k), act[k].at[0:3])
        half = act[k].at[pl.ds(core * 4, 4)]
        send(slot(5, k), half, half, core_dev)
        pending.append((slot(5, k), act[k].at[0:4]))
        wait(1, slot(13, k), hidden_all[k].at[0:3])
        half = hidden_all[k].at[pl.ds(core * 4, 4)]
        send(slot(14, k), half, half, core_dev)
        pending.append((slot(14, k), hidden_all[k].at[0:4]))

    def rebuild(k):
        wait(1, slot(5, k), act[k].at[0:4])
        wait(1, slot(14, k), hidden_all[k].at[0:4])
        part = nt(act[k][...].reshape(chunk_tokens[k], both), w_dec[...]) - jnp.dot(
            hidden_all[k][...].reshape(chunk_tokens[k], 2 * hid), w_down[...], preferred_element_type=F32
        )
        err_part[k][...] = part.astype(BF16).reshape(slots, ROWS[k], -1)
        for s, dev in zip(y_at, y_dev):
            send(slot(6, k), err_part[k].at[s], err_recv[k].at[yy], dev)
        pending.append((slot(6, k), err_part[k].at[0:7]))
        err_recv[k][yy] = err_part[k][yy]

    def sum_y(k):
        wait(1, slot(6, k), err_recv[k].at[0:7])
        total = err_recv[k][0].astype(F32)
        for s in range(1, 8):
            total = total + err_recv[k][s].astype(F32)
        err_xl[k][xl] = total.astype(BF16)
        for dev in xl_dev:
            send(slot(7, k), err_xl[k].at[xl], err_xl[k].at[xl], dev)
        pending.append((slot(7, k), err_xl[k].at[0:7]))

    def sum_xl(k):
        wait(1, slot(7, k), err_xl[k].at[0:7])
        total = err_xl[k][0].astype(F32)
        for s in range(1, 8):
            total = total + err_xl[k][s].astype(F32)
        errors[k][yy] = total.astype(BF16)
        for dev in y_dev:
            send(slot(8, k), errors[k].at[yy], errors[k].at[yy], dev)
        pending.append((slot(8, k), errors[k].at[0:7]))

    def back_matmul(k):
        wait(1, slot(8, k), errors[k].at[0:7])
        e = errors[k][...].reshape(chunk_tokens[k], 2 * cols)
        back = jnp.dot(e, w_dec[...], preferred_element_type=F32)
        back_mine[k][...] = back.astype(BF16).reshape(slots, ROWS[k], both)
        send(slot(9, k), back_mine[k].at[pl.ds((1 - core) * 4, 4)], back_core[k], core_dev)
        pending.append((slot(9, k), back_core[k]))

    def back_to_z(k):
        wait(1, slot(9, k), back_core[k])
        for z, dev in zip(z_at, z_dev):
            back_z[k][z] = (
                back_mine[k][core * 4 + z].astype(F32) + back_core[k][z].astype(F32)
            ).astype(BF16)
            send(slot(10, k), back_z[k].at[z], back_recv[k].at[zh], dev)
        pending.append((slot(10, k), back_z[k].at[0:3]))
        back_recv[k][zh] = (
            back_mine[k][mine].astype(F32) + back_core[k][zh].astype(F32)
        ).astype(BF16)
        errors_t[:, first_token[k] : first_token[k] + chunk_tokens[k]] = errors[k][...].reshape(chunk_tokens[k], 2 * cols).T

    def pre_grad(k):
        wait(1, slot(10, k), back_recv[k].at[0:3])
        total = back_recv[k][0].astype(F32)
        for z in range(1, 4):
            total = total + back_recv[k][z].astype(F32)
        grads[k][mine] = jnp.where(
            act[k][mine].astype(F32) > 0, scale * (total + sparsity_weight), 0.0
        ).astype(BF16)
        for dev in z_dev:
            send(slot(11, k), grads[k].at[mine], grads[k].at[mine], dev)
        pending.append((slot(11, k), grads[k].at[0:3]))

    def grads_to_core(k):
        wait(1, slot(11, k), grads[k].at[0:3])
        half = grads[k].at[pl.ds(core * 4, 4)]
        send(slot(12, k), half, half, core_dev)
        pending.append((slot(12, k), grads[k].at[0:4]))

    def encoder_grads(k):
        wait(1, slot(12, k), grads[k].at[0:4])
        g = grads[k][...].reshape(chunk_tokens[k], both)
        ones = jnp.ones((8, chunk_tokens[k]), BF16)
        for l in range(layers):
            g_layer = g[:, l * feats : (l + 1) * feats]
            x_t = normed_t[l * cols : (l + 1) * cols, first_token[k] : first_token[k] + chunk_tokens[k]]
            part = jnp.dot(x_t, g_layer, preferred_element_type=F32)
            if k > 0:
                part = part + enc_sum[l]
            if k < chunks - 1:
                enc_sum[l] = part
            else:
                grad_encoder[l] = part.astype(BF16)
            column = jnp.dot(ones, g_layer, preferred_element_type=F32)[0:1]
            if k > 0:
                column = column + grad_bias[l : l + 1, :]
            grad_bias[l : l + 1, :] = column

    def decoder_grads():
        first = second = None
        for k in range(chunks):
            a = act[k][...].reshape(chunk_tokens[k], both)
            e = errors_t[:, first_token[k] : first_token[k] + chunk_tokens[k]]
            one = jnp.dot(e, a[:, 0:feats], preferred_element_type=F32)
            two = jnp.dot(e[cols : 2 * cols], a[:, feats:both], preferred_element_type=F32)
            first, second = (one, two) if k == 0 else (first + one, second + two)
        grad_decoder[0] = (first[0:cols] * scale).astype(BF16)
        grad_decoder[1] = (first[cols : 2 * cols] * scale).astype(BF16)
        grad_decoder[2] = (second * scale).astype(BF16)

    stages = (
        pre_matmul, pre_to_z, activate, act_to_core, rebuild, sum_y, sum_xl,
        back_matmul, back_to_z, pre_grad, grads_to_core, encoder_grads,
    )
    order = sorted(
        (STAGE_TIMES[j] + CHUNK_STEP * k, k, j) for k in range(chunks) for j in range(len(stages))
    )
    for _, k, j in order:
        stages[j](k)
        if (k, j) == (chunks - 1, 8):
            decoder_grads()

    for i, ref in pending:
        wait(0, i, ref)


def step(residual, norm_gain, gate_weight, up_weight, down_weight, encoder, encoder_bias, decoder, width):
    layers, local, cols = residual.shape
    feats = encoder.shape[1]
    hid = gate_weight.shape[2]
    chunks, slots = len(ROWS), 8
    tokens = slots * sum(ROWS)
    both, wide, hidden, gate_up = layers * feats, layers * cols, layers * hid, 2 * layers * hid
    vm = pltpu.VMEM
    scratch = [
        vm((8, 8, 128), F32),
        vm((16, cols), F32),
        vm((16, 16, cols), BF16),
        vm((16 * local, wide), F32),
        vm((wide, both), BF16),
        vm((wide, both), BF16),
        vm((gate_up, wide), BF16),
        vm((hidden, wide), BF16),
        vm((layers, hid, cols), BF16),
        vm((layers, hid, cols), BF16),
        vm((layers, hid, cols), BF16),
        vm((wide, tokens), BF16),
        vm((wide, tokens), BF16),
        vm((layers, cols, feats), F32),
        pltpu.SemaphoreType.DMA((2, 2 + chunks * 16)),
        pltpu.SemaphoreType.DMA((8,)),
    ]
    scratch += [vm((4, 2 * rows, wide), BF16) for rows in ROWS]
    for lead, last, dtype in (
        (slots, both, F32), (4, both, F32), (4, both, F32), (4, both, F32),
        (slots, gate_up, BF16), (4, gate_up, BF16), (4, gate_up, BF16), (4, gate_up, BF16),
        (slots, both, BF16), (slots, hidden, BF16),
        (slots, wide, BF16), (slots, wide, BF16), (8, wide, BF16), (slots, wide, BF16),
        (slots, both, BF16), (4, both, BF16), (4, both, BF16), (4, both, BF16), (slots, both, BF16),
    ):
        scratch += [vm((lead, rows, last), dtype) for rows in ROWS]
    spec = pl.BlockSpec(memory_space=pltpu.VMEM)
    anywhere = pl.BlockSpec(memory_space=pl.ANY)
    grad_encoder, grad_bias, grad_decoder = pl.pallas_call(
        functools.partial(kernel, width),
        out_shape=(
            jax.ShapeDtypeStruct((layers, cols, feats), BF16),
            jax.ShapeDtypeStruct(encoder_bias.shape, F32),
            jax.ShapeDtypeStruct((decoder.shape[0], cols, feats), BF16),
        ),
        in_specs=[spec, spec, anywhere, anywhere, anywhere, anywhere, spec, anywhere],
        out_specs=(spec,) * 3,
        scratch_shapes=scratch,
        compiler_params=pltpu.CompilerParams(
            collective_id=0, has_side_effects=True, vmem_limit_bytes=56 * 2**20
        ),
        name="train_step",
    )(
        residual.swapaxes(0, 1), norm_gain, gate_weight.swapaxes(1, 2), up_weight.swapaxes(1, 2),
        down_weight, encoder.swapaxes(1, 2), encoder_bias, decoder.swapaxes(1, 2),
    )
    return grad_encoder.swapaxes(1, 2), grad_bias, grad_decoder.swapaxes(1, 2)


def solution(mesh):
    def body(*args):
        return step(*args, width=args[0].shape[2] * mesh.shape["mp"])

    return jax.shard_map(
        body,
        mesh=mesh,
        in_specs=(
            P(None, "feat", "mp"),
            P(None, "mp"),
            P(None, "mp", "feat"),
            P(None, "mp", "feat"),
            P(None, "feat", "mp"),
            P(None, "feat", "mp"),
            P(None, "feat"),
            P(None, "feat", "mp"),
        ),
        out_specs=(P(None, "feat", "mp"), P(None, "feat"), P(None, "feat", "mp")),
        check_vma=False,
    )
```
